32 devices in a mesh: col: 4 (over y, core), row: 4 (over z), tok: 2 (over x).
Axes of the slice: x: 2, y: 2, z: 4, core: 2. Of those that a mesh axis runs over, the one named last changes fastest.
Arguments:
- queries: bfloat16 [256, 16384], P('tok', ('col', 'row')), may hold values from -512 to 512
- key_rows: bfloat16 [256, 16384], P('tok', ('col', 'row')), may hold values from -12 to 12
- values: bfloat16 [256, 16384], P('tok', ('col', 'row')), may hold values from -6 to 6
- code_first: int32 [16384, 2048], P(('row', 'tok'), 'col'), may hold values from 0 to 255
- code_second: int32 [16384, 2048], P(('row', 'tok'), 'col'), may hold values from 0 to 255
- book_first: bfloat16 [256, 8], replicated, may hold values from -0.59765625 to 0.59765625
- book_second: bfloat16 [256, 8], replicated, may hold values from -0.59765625 to 0.59765625
- scales: float32 [16384], P(('row', 'tok')), may hold values from 0.015 to 0.15
- target: bfloat16 [256, 16384], P(None, ('row', 'tok')), may hold values from -2 to 2
Outputs:
- misfit: bfloat16 [256, 16384], P(None, ('row', 'tok'))
- grad_scales: float32 [16384], P(('row', 'tok'))
- grad_books: float32 [2, 256, 8], replicated
The draws below stay inside these ranges and needn't reach their ends.
All inputs are finite; a program needn't handle non-finite values.
Results may differ from the reference program's by a relative error of at most 0.0053.
Values may be sent and summed in bfloat16 or wider, within the bound.
A program may use at most 128 MiB of HBM per device.

```python
import math
import jax
import jax.numpy as jnp
from jax import lax

HEADS = 128
HEAD_DIM = 128
ENTRIES = 256
GROUP = 8
D = 16384
TOKENS = 256


def draw_pair(key):
    base = jax.random.fold_in(key, 41)
    key_query, key_key = jax.random.split(base, 2)
    key_field = jax.random.normal(key_key, (TOKENS, HEADS, HEAD_DIM), jnp.float32)
    query_field = jax.random.normal(key_query, (TOKENS, HEADS, HEAD_DIM), jnp.float32)
    key_field = jnp.clip(key_field, -6.0, 6.0)
    query_field = jnp.clip(query_field, -6.0, 6.0)
    return (query_field.reshape(TOKENS, HEADS * HEAD_DIM), key_field.reshape(TOKENS, HEADS * HEAD_DIM))


def draw_queries(key, part):
    return draw_pair(key)[0].astype(jnp.bfloat16)


def draw_key_rows(key, part):
    return draw_pair(key)[1].astype(jnp.bfloat16)


def with_ends(drawn, own_key, low, largest):
    spot = [jax.random.randint(jax.random.fold_in(own_key, axis), (), 0, length) for axis, length in enumerate(drawn.shape)]
    main_axis = drawn.shape.index(max(drawn.shape))
    beside = spot[:main_axis] + [(spot[main_axis] + 1) % drawn.shape[main_axis]] + spot[main_axis + 1:]
    return drawn.at[tuple(spot)].set(low).at[tuple(beside)].set(largest)


def shard_levels(stream_key, shape, cuts, least, top_value):
    def one(axis_at, shards_of):
        heights = jax.random.uniform(jax.random.fold_in(jax.random.fold_in(stream_key, 6), axis_at), (shards_of,), jnp.float32, least / len(cuts), top_value / len(cuts))
        return jnp.repeat(jnp.exp(heights), shape[axis_at] // shards_of).reshape((-1,) + (1,) * (len(shape) - axis_at - 1))

    factor_of = one(*cuts[0])
    for cut in cuts[1:]:
        factor_of = factor_of * one(*cut)
    return factor_of


def noise(stream_key, extent, deviation, reach, cuts=(), kind=jnp.bfloat16):
    level = shard_levels(stream_key, extent, cuts, -0.22, 0.18) if cuts else 1.0
    entries = jax.random.normal(stream_key, extent, jnp.float32) * deviation * level
    return jnp.minimum(jnp.maximum(entries, -reach), reach).astype(kind)


def setup_inputs(seed: int = 0) -> dict:
    seeds = jax.random.split(jax.random.key(seed), 10)
    return {
        "queries": draw_queries(jax.random.fold_in(seeds[9], 71), 0),
        "key_rows": draw_key_rows(jax.random.fold_in(seeds[9], 71), 0),
        "values": noise(seeds[2], (TOKENS, D), 1.0, 6.0, ((0, 2), (1, 16))),
        "code_first": with_ends(jax.random.randint(seeds[3], (D, D // GROUP), 0, ENTRIES), jax.random.fold_in(seeds[3], 1), 0, ENTRIES - 1).astype(jnp.int32),
        "code_second": with_ends(jax.random.randint(seeds[4], (D, D // GROUP), 0, ENTRIES), jax.random.fold_in(seeds[4], 1), 0, ENTRIES - 1).astype(jnp.int32),
        "book_first": noise(seeds[5], (ENTRIES, GROUP), 0.1, 0.59765625),
        "book_second": noise(seeds[6], (ENTRIES, GROUP), 0.1, 0.59765625),
        "scales": jnp.clip(jnp.exp(math.log(0.15) - 2.3025852 * jax.random.uniform(seeds[7], (D,), jnp.float32) ** shard_levels(seeds[7], (D,), ((0, 8),), -0.2, 0.2)), 0.015, 0.15),
        "target": noise(seeds[8], (TOKENS, D), 0.3, 2.0, ((1, 8),)),
    }


def attend_head(operands):
    query_head, key_head, value_head = operands
    scores = jnp.dot(query_head, key_head.T, preferred_element_type=jnp.float32) / math.sqrt(HEAD_DIM)
    places = jnp.arange(scores.shape[0], dtype=jnp.int32)
    allowed = places[None, :] <= places[:, None]
    row_max = lax.optimization_barrier(jnp.max(jnp.where(allowed, scores, -jnp.inf), axis=1, keepdims=True))
    exponent = jnp.where(allowed, jnp.exp(scores - row_max), 0.0)
    row_sum = lax.optimization_barrier(jnp.sum(exponent, axis=1, keepdims=True))
    probs = exponent.astype(jnp.bfloat16)
    return jnp.dot(probs, value_head, preferred_element_type=jnp.float32) / row_sum

def split_heads(matrix):
    return matrix.reshape(TOKENS, HEADS, HEAD_DIM).transpose(1, 0, 2)

def reference(queries, key_rows, values, code_first, code_second, book_first, book_second, scales, target):
    heads_out = lax.map(attend_head, (split_heads(queries), split_heads(key_rows), split_heads(values)))
    attended = heads_out.transpose(1, 0, 2).reshape(TOKENS, D).astype(jnp.bfloat16)
    block_rows = math.gcd(D, 1024)
    count_blocks = D // block_rows
    first_book = book_first.astype(jnp.float32)
    second_book = book_second.astype(jnp.float32)

    def project(books_sum, operands):
        first_codes, second_codes, block_scales, block_target = operands
        unscaled = (jnp.take(first_book, first_codes, axis=0) + jnp.take(second_book, second_codes, axis=0)).reshape(block_rows, D)
        weight = (block_scales[:, None] * unscaled).astype(jnp.bfloat16)
        output = lax.dot_general(attended, weight, (((1,), (1,)), ((), ())), preferred_element_type=jnp.float32)
        misfit = (output - block_target.astype(jnp.float32)).astype(jnp.bfloat16)
        weight_grad = lax.dot_general(misfit, attended, (((0,), (0,)), ((), ())), preferred_element_type=jnp.float32) / TOKENS
        scale_grad = lax.optimization_barrier(jnp.sum(weight_grad * unscaled, axis=1))
        scaled = (block_scales[:, None] * weight_grad).reshape(-1, GROUP)
        book_terms = jnp.stack([jax.ops.segment_sum(scaled, first_codes.reshape(-1), ENTRIES), jax.ops.segment_sum(scaled, second_codes.reshape(-1), ENTRIES)])
        return (books_sum + book_terms, (misfit, scale_grad))
    targets_split = target.reshape(TOKENS, count_blocks, block_rows).transpose(1, 0, 2)
    initial = jnp.zeros((2, ENTRIES, GROUP), jnp.float32)
    grad_books, (misfit_blocks, scale_blocks) = lax.scan(project, initial, (code_first.reshape(count_blocks, block_rows, D // GROUP), code_second.reshape(count_blocks, block_rows, D // GROUP), scales.reshape(count_blocks, block_rows), targets_split))
    misfit = misfit_blocks.transpose(1, 0, 2).reshape(TOKENS, D)
    return (misfit, scale_blocks.reshape(D), grad_books)
```

```python
import functools
import math

import jax
import jax.numpy as jnp
from jax import lax
from jax.experimental import pallas as pl
from jax.experimental.pallas import tpu as pltpu
from jax.sharding import PartitionSpec as P

HEAD_DIM = 128
ENTRIES = 256
GROUP = 8
LANES = 128
LOW = 8
HIGH = ENTRIES // LOW
OCTET = 8
VMEM_LIMIT = 48 * 1024 * 1024


def look_up(table, codes):
    place = codes & (LANES - 1)
    lower = jnp.take_along_axis(table[0], place, axis=1, mode="promise_in_bounds")
    upper = jnp.take_along_axis(table[1], place, axis=1, mode="promise_in_bounds")
    return jnp.where((codes & LANES) != 0, upper, lower)


def dequantize_kernel(first_ref, second_ref, books_ref, scales_ref, weight_ref, codes_ref):
    codes_ref[...] = (first_ref[...] + second_ref[...] * ENTRIES).T
    groups, rows = codes_ref.shape
    tables = [
        [books_ref[book, :, half * LANES : (half + 1) * LANES] for half in range(2)]
        for book in range(2)
    ]

    @pl.loop(0, groups // 2, unroll=4)
    def _(pair):
        parts = []
        for side in range(2):
            row = codes_ref[pl.ds(pair * 2 + side, 1), :]
            pieces = []
            for start in range(0, rows, LANES):
                codes = jnp.broadcast_to(row[:, start : start + LANES], (GROUP, LANES))
                unscaled = look_up(tables[0], codes) + look_up(tables[1], codes >> 8)
                pieces.append(unscaled * scales_ref[:, start : start + LANES])
            parts.append(jnp.concatenate(pieces, axis=1))
        rows16 = pl.ds(pl.multiple_of(pair * 16, 16), 16)
        weight_ref[rows16, :] = jnp.concatenate(parts, axis=0).astype(jnp.bfloat16)


def dequantize(code_first, code_second, books, scales):
    rows, groups = code_first.shape
    block = math.gcd(rows, 512)
    return pl.pallas_call(
        dequantize_kernel,
        grid=(groups // LANES, rows // block),
        in_specs=[
            pl.BlockSpec((block, LANES), lambda g, o: (o, g)),
            pl.BlockSpec((block, LANES), lambda g, o: (o, g)),
            pl.BlockSpec((2, GROUP, ENTRIES), lambda g, o: (0, 0, 0)),
            pl.BlockSpec((1, block), lambda g, o: (0, o)),
        ],
        out_specs=[
            pl.BlockSpec((LANES * GROUP, block), lambda g, o: (g, o)),
            pl.BlockSpec((LANES, block), lambda g, o: (g, o)),
        ],
        out_shape=[
            jax.ShapeDtypeStruct((groups * GROUP, rows), jnp.bfloat16),
            jax.ShapeDtypeStruct((groups, rows), jnp.int32),
        ],
        compiler_params=pltpu.CompilerParams(vmem_limit_bytes=VMEM_LIMIT),
        cost_estimate=pl.CostEstimate(
            flops=32 * rows * groups * GROUP,
            bytes_accessed=rows * groups * (12 + 2 * GROUP),
            transcendentals=0,
        ),
        name="dequantize",
    )(code_first, code_second, books, scales)


def bin_kernel(chunk, attended_ref, misfit_ref, codes_ref, scales_ref, total_ref, grad_ref):
    @pl.when(pl.program_id(0) == 0)
    def _():
        total_ref[...] = jnp.zeros_like(total_ref)

    rows = misfit_ref.shape[1]
    groups = codes_ref.shape[0]
    width = OCTET * GROUP

    @pl.loop(0, rows // chunk)
    def _(part):
        cols = pl.ds(pl.multiple_of(part * chunk, chunk), chunk)
        grad_ref[...] = (
            jnp.dot(
                attended_ref[...], misfit_ref[:, cols], preferred_element_type=jnp.float32
            )
            * scales_ref[:, cols]
        ).astype(jnp.bfloat16)

        @pl.loop(0, groups // OCTET, unroll=2)
        def _(octet):
            grad = grad_ref[pl.ds(pl.multiple_of(octet * width, width), width), :]
            places = lax.broadcasted_iota(jnp.int32, (HIGH, chunk), 0).astype(jnp.bfloat16)
            lines = [codes_ref[pl.ds(octet * OCTET + g, 1), cols] for g in range(OCTET)]
            for book in range(2):
                own = [(line >> (8 * book)) & (ENTRIES - 1) for line in lines]
                low = jnp.concatenate(
                    [jnp.broadcast_to(code & (LOW - 1), (GROUP, chunk)) for code in own], axis=0
                ).astype(jnp.bfloat16)
                left = jnp.concatenate(
                    [
                        jnp.where(low == jnp.bfloat16(k), grad, jnp.bfloat16(0))
                        for k in range(LOW)
                    ],
                    axis=0,
                )
                right = jnp.concatenate(
                    [
                        jnp.where(
                            jnp.broadcast_to(code // LOW, (HIGH, chunk)).astype(jnp.bfloat16)
                            == places,
                            jnp.bfloat16(1),
                            jnp.bfloat16(0),
                        )
                        for code in own
                    ],
                    axis=0,
                )
                total_ref[book] += lax.dot_general(
                    left, right, (((1,), (1,)), ((), ())), preferred_element_type=jnp.float32
                )


def bin_grads(attended, misfit, codes, scales):
    groups, rows = codes.shape
    tokens = misfit.shape[0]
    block = math.gcd(groups, 32)
    chunk = math.gcd(rows, 512)
    total = pl.pallas_call(
        functools.partial(bin_kernel, chunk),
        grid=(groups // block,),
        in_specs=[
            pl.BlockSpec((block * GROUP, tokens), lambda g: (g, 0)),
            pl.BlockSpec((tokens, rows), lambda g: (0, 0)),
            pl.BlockSpec((block, rows), lambda g: (g, 0)),
            pl.BlockSpec((1, rows), lambda g: (0, 0)),
        ],
        out_specs=pl.BlockSpec(
            (2, LOW * OCTET * GROUP, OCTET * HIGH), lambda g: (0, 0, 0)
        ),
        out_shape=jax.ShapeDtypeStruct((2, LOW * OCTET * GROUP, OCTET * HIGH), jnp.float32),
        scratch_shapes=[pltpu.VMEM((block * GROUP, chunk), jnp.bfloat16)],
        compiler_params=pltpu.CompilerParams(vmem_limit_bytes=VMEM_LIMIT),
        cost_estimate=pl.CostEstimate(
            flops=4 * rows * groups * LOW * GROUP * OCTET * HIGH,
            bytes_accessed=rows * groups * 4,
            transcendentals=0,
        ),
        name="bin_grads",
    )(attended, misfit, codes, scales)
    split = total.reshape(2, LOW, OCTET, GROUP, OCTET, HIGH)
    same = jnp.eye(OCTET, dtype=jnp.float32)[None, None, :, None, :, None]
    kept = jnp.sum(split * same, axis=(2, 4))
    return kept.transpose(0, 3, 1, 2).reshape(2, ENTRIES, GROUP)


def attend(queries, key_rows, values):
    tok_rows, width = queries.shape
    heads_here = width // HEAD_DIM
    query_heads = queries.reshape(tok_rows, heads_here, HEAD_DIM)
    query_place = lax.axis_index("tok") * tok_rows + lax.iota(jnp.int32, tok_rows)
    key_piece = lax.all_gather(key_rows, "tok", axis=0, tiled=True)
    value_piece = lax.all_gather(values, "tok", axis=0, tiled=True)
    length = key_piece.shape[0]
    key_heads = key_piece.reshape(length, heads_here, HEAD_DIM)
    value_heads = value_piece.reshape(length, heads_here, HEAD_DIM)
    scores = jnp.einsum(
        "qhd,khd->hqk", query_heads, key_heads, preferred_element_type=jnp.float32
    ) / math.sqrt(HEAD_DIM)
    key_place = lax.iota(jnp.int32, length)
    allowed = (key_place[None, :] <= query_place[:, None])[None]
    peak = jnp.max(jnp.where(allowed, scores, -jnp.inf), axis=-1)
    exponent = jnp.where(allowed, jnp.exp(scores - peak[..., None]), 0.0)
    probs = exponent.astype(jnp.bfloat16)
    row_sum = jnp.sum(exponent, axis=-1)
    weighted = jnp.einsum("hqk,khd->hqd", probs, value_heads, preferred_element_type=jnp.float32)
    return (weighted / row_sum[..., None]).transpose(0, 2, 1).reshape(width, tok_rows).astype(
        jnp.bfloat16
    )


def local(
    queries, key_rows, values, code_first, code_second, book_first, book_second, scales, target
):
    books = jnp.stack([book_first.T, book_second.T]).astype(jnp.float32)
    weight, codes = dequantize(code_first, code_second, books, scales[None])
    attended = attend(queries, key_rows, values)
    head_cols = lax.all_gather(attended, "row", axis=0, tiled=True)
    gathered = lax.all_gather(head_cols, "tok", axis=1, tiled=True)
    partial_value = lax.dot_general(
        gathered, weight, (((0,), (0,)), ((), ())), preferred_element_type=jnp.float32
    )
    summed_out = lax.psum(partial_value, "col")
    misfit = (summed_out - target.astype(jnp.float32)).astype(jnp.bfloat16)
    tokens = misfit.shape[0]
    grad_scales = jnp.sum(misfit.astype(jnp.float32) * summed_out, axis=0) / (scales * tokens)
    grad_books = bin_grads(gathered, misfit, codes, (scales / tokens)[None])
    grad_books = lax.psum(grad_books, ("col", "row", "tok"))
    return (misfit, grad_scales, grad_books)


def solution(mesh):
    in_specs = (
        P("tok", ("col", "row")),
        P("tok", ("col", "row")),
        P("tok", ("col", "row")),
        P(("row", "tok"), "col"),
        P(("row", "tok"), "col"),
        P(),
        P(),
        P(("row", "tok")),
        P(None, ("row", "tok")),
    )
    out_specs = (P(None, ("row", "tok")), P(("row", "tok")), P())
    return jax.shard_map(local, mesh=mesh, in_specs=in_specs, out_specs=out_specs, check_vma=False)
```

```python
import functools
import math

import jax
import jax.numpy as jnp
from jax import lax
from jax.experimental import pallas as pl
from jax.experimental.pallas import tpu as pltpu
from jax.sharding import PartitionSpec as P

HEAD_DIM = 128
ENTRIES = 256
GROUP = 8
LANES = 128
LOW = 8
HIGH = ENTRIES // LOW
OCTET = 8
VMEM_LIMIT = 48 * 1024 * 1024


def look_up(table, codes):
    place = codes & (LANES - 1)
    lower = jnp.take_along_axis(table[0], place, axis=1, mode="promise_in_bounds")
    upper = jnp.take_along_axis(table[1], place, axis=1, mode="promise_in_bounds")
    return jnp.where((codes & LANES) != 0, upper, lower)


def dequantize_kernel(first_ref, second_ref, books_ref, scales_ref, weight_ref, codes_ref):
    codes_ref[...] = (first_ref[...] + second_ref[...] * ENTRIES).T
    groups, rows = codes_ref.shape
    tables = [
        [books_ref[book, :, half * LANES : (half + 1) * LANES] for half in range(2)]
        for book in range(2)
    ]

    @pl.loop(0, groups // 2, unroll=4)
    def _(pair):
        parts = []
        for side in range(2):
            row = codes_ref[pl.ds(pair * 2 + side, 1), :]
            pieces = []
            for start in range(0, rows, LANES):
                codes = jnp.broadcast_to(row[:, start : start + LANES], (GROUP, LANES))
                unscaled = look_up(tables[0], codes) + look_up(tables[1], codes >> 8)
                pieces.append(unscaled * scales_ref[:, start : start + LANES])
            parts.append(jnp.concatenate(pieces, axis=1))
        rows16 = pl.ds(pl.multiple_of(pair * 16, 16), 16)
        weight_ref[rows16, :] = jnp.concatenate(parts, axis=0).astype(jnp.bfloat16)


def dequantize(code_first, code_second, books, scales, part, parts):
    groups = code_first.shape[1]
    rows = code_first.shape[0] // parts
    block = math.gcd(rows, 512)
    first = part * (rows // block)
    return pl.pallas_call(
        dequantize_kernel,
        grid=(groups // LANES, rows // block),
        in_specs=[
            pl.BlockSpec((block, LANES), lambda g, o: (first + o, g)),
            pl.BlockSpec((block, LANES), lambda g, o: (first + o, g)),
            pl.BlockSpec((2, GROUP, ENTRIES), lambda g, o: (0, 0, 0)),
            pl.BlockSpec((1, block), lambda g, o: (0, first + o)),
        ],
        out_specs=[
            pl.BlockSpec((LANES * GROUP, block), lambda g, o: (g, o)),
            pl.BlockSpec((LANES, block), lambda g, o: (g, o)),
        ],
        out_shape=[
            jax.ShapeDtypeStruct((groups * GROUP, rows), jnp.bfloat16),
            jax.ShapeDtypeStruct((groups, rows), jnp.int32),
        ],
        compiler_params=pltpu.CompilerParams(vmem_limit_bytes=VMEM_LIMIT),
        cost_estimate=pl.CostEstimate(
            flops=32 * rows * groups * GROUP,
            bytes_accessed=rows * groups * (12 + 2 * GROUP),
            transcendentals=0,
        ),
        name="dequantize",
    )(code_first, code_second, books, scales)


def bin_kernel(chunk, attended_ref, misfit_ref, codes_ref, scales_ref, total_ref, grad_ref):
    @pl.when(pl.program_id(0) == 0)
    def _():
        total_ref[...] = jnp.zeros_like(total_ref)

    rows = misfit_ref.shape[1]
    groups = codes_ref.shape[0]
    width = OCTET * GROUP

    @pl.loop(0, rows // chunk)
    def _(part):
        cols = pl.ds(pl.multiple_of(part * chunk, chunk), chunk)
        grad_ref[...] = (
            jnp.dot(
                attended_ref[...], misfit_ref[:, cols], preferred_element_type=jnp.float32
            )
            * scales_ref[:, cols]
        ).astype(jnp.bfloat16)

        @pl.loop(0, groups // OCTET, unroll=2)
        def _(octet):
            grad = grad_ref[pl.ds(pl.multiple_of(octet * width, width), width), :]
            places = lax.broadcasted_iota(jnp.int32, (HIGH, chunk), 0).astype(jnp.bfloat16)
            lines = [codes_ref[pl.ds(octet * OCTET + g, 1), cols] for g in range(OCTET)]
            for book in range(2):
                own = [(line >> (8 * book)) & (ENTRIES - 1) for line in lines]
                low = jnp.concatenate(
                    [jnp.broadcast_to(code & (LOW - 1), (GROUP, chunk)) for code in own], axis=0
                ).astype(jnp.bfloat16)
                left = jnp.concatenate(
                    [
                        jnp.where(low == jnp.bfloat16(k), grad, jnp.bfloat16(0))
                        for k in range(LOW)
                    ],
                    axis=0,
                )
                right = jnp.concatenate(
                    [
                        jnp.where(
                            jnp.broadcast_to(code // LOW, (HIGH, chunk)).astype(jnp.bfloat16)
                            == places,
                            jnp.bfloat16(1),
                            jnp.bfloat16(0),
                        )
                        for code in own
                    ],
                    axis=0,
                )
                total_ref[book] += lax.dot_general(
                    left, right, (((1,), (1,)), ((), ())), preferred_element_type=jnp.float32
                )


def bin_grads(attended, misfit, codes, scales):
    groups, rows = codes.shape
    tokens = misfit.shape[0]
    block = math.gcd(groups, 32)
    chunk = math.gcd(rows, 512)
    return pl.pallas_call(
        functools.partial(bin_kernel, chunk),
        grid=(groups // block,),
        in_specs=[
            pl.BlockSpec((block * GROUP, tokens), lambda g: (g, 0)),
            pl.BlockSpec((tokens, rows), lambda g: (0, 0)),
            pl.BlockSpec((block, rows), lambda g: (g, 0)),
            pl.BlockSpec((1, rows), lambda g: (0, 0)),
        ],
        out_specs=pl.BlockSpec(
            (2, LOW * OCTET * GROUP, OCTET * HIGH), lambda g: (0, 0, 0)
        ),
        out_shape=jax.ShapeDtypeStruct((2, LOW * OCTET * GROUP, OCTET * HIGH), jnp.float32),
        scratch_shapes=[pltpu.VMEM((block * GROUP, chunk), jnp.bfloat16)],
        compiler_params=pltpu.CompilerParams(vmem_limit_bytes=VMEM_LIMIT),
        cost_estimate=pl.CostEstimate(
            flops=4 * rows * groups * LOW * GROUP * OCTET * HIGH,
            bytes_accessed=rows * groups * 4,
            transcendentals=0,
        ),
        name="bin_grads",
    )(attended, misfit, codes, scales)

def fold_book(total):
    groups_at = lax.broadcasted_iota(jnp.int32, total.shape, 0) // GROUP % OCTET
    lanes_at = lax.broadcasted_iota(jnp.int32, total.shape, 1) // HIGH
    kept = jnp.where(groups_at == lanes_at, total, 0.0)
    kept = jnp.sum(kept.reshape(LOW, OCTET, GROUP, OCTET * HIGH), axis=1)
    kept = kept.reshape(LOW * GROUP, OCTET * HIGH)
    kept = kept[:, :LANES] + kept[:, LANES:]
    kept = kept + pltpu.roll(kept, 2 * HIGH, 1)
    return kept + pltpu.roll(kept, HIGH, 1)


def sum_kernel(axes, *refs):
    count = len(axes)
    total_refs, out_ref = refs[: -3 * count - 1], refs[-3 * count - 1]
    slots, sends, arrivals = (
        refs[-3 * count : -2 * count],
        refs[-2 * count : -count],
        refs[-count:],
    )
    barrier = pltpu.get_barrier_semaphore()
    peers = 0
    for name, size in axes:
        me = lax.axis_index(name)
        for ahead in range(1, size):
            pl.semaphore_signal(
                barrier,
                inc=1,
                device_id={name: lax.rem(me + ahead, size)},
                device_id_type=pl.DeviceIdType.MESH,
            )
            peers += 1
    folded = []
    for book in range(2):
        total = total_refs[0][book]
        for ref in total_refs[1:]:
            total = total + ref[book]
        folded.append(fold_book(total))
    lane = lax.broadcasted_iota(jnp.int32, folded[0].shape, 1)
    current = jnp.where(lane < HIGH, folded[0], folded[1])
    pl.semaphore_wait(barrier, peers)
    for stage, (name, size) in enumerate(axes):
        me = lax.axis_index(name)
        slots[stage][me] = current
        copies = []
        for ahead in range(1, size):
            copy = pltpu.make_async_remote_copy(
                src_ref=slots[stage].at[me],
                dst_ref=slots[stage].at[me],
                send_sem=sends[stage].at[ahead],
                recv_sem=arrivals[stage].at[ahead],
                device_id={name: lax.rem(me + ahead, size)},
                device_id_type=pl.DeviceIdType.MESH,
            )
            copy.start()
            copies.append(copy)
        for copy in copies:
            copy.wait()
        current = slots[stage][0]
        for place in range(1, size):
            current = current + slots[stage][place]
    out_ref[...] = current


def sum_books(totals):
    axes = [(name, lax.axis_size(name)) for name in ("col", "row", "tok")]
    shape = (LOW * GROUP, LANES)
    summed = pl.pallas_call(
        functools.partial(sum_kernel, axes),
        in_specs=[pl.BlockSpec(memory_space=pltpu.VMEM)] * len(totals),
        out_specs=pl.BlockSpec(memory_space=pltpu.VMEM),
        out_shape=jax.ShapeDtypeStruct(shape, jnp.float32),
        scratch_shapes=[pltpu.VMEM((size, *shape), jnp.float32) for _, size in axes]
        + [pltpu.SemaphoreType.DMA((size,)) for _, size in axes] * 2,
        compiler_params=pltpu.CompilerParams(
            collective_id=0, has_side_effects=True, vmem_limit_bytes=VMEM_LIMIT
        ),
        name="sum_books",
    )(*totals)
    split = summed[:, : 2 * HIGH].reshape(LOW, GROUP, 2, HIGH)
    return split.transpose(2, 3, 0, 1).reshape(2, ENTRIES, GROUP)


def attend(queries, key_rows, values):
    tok_rows, width = queries.shape
    heads_here = width // HEAD_DIM
    query_heads = queries.reshape(tok_rows, heads_here, HEAD_DIM)
    query_place = lax.axis_index("tok") * tok_rows + lax.iota(jnp.int32, tok_rows)
    key_piece = lax.all_gather(key_rows, "tok", axis=0, tiled=True)
    value_piece = lax.all_gather(values, "tok", axis=0, tiled=True)
    length = key_piece.shape[0]
    key_heads = key_piece.reshape(length, heads_here, HEAD_DIM)
    value_heads = value_piece.reshape(length, heads_here, HEAD_DIM)
    scores = jnp.einsum(
        "qhd,khd->hqk", query_heads, key_heads, preferred_element_type=jnp.float32
    ) / math.sqrt(HEAD_DIM)
    key_place = lax.iota(jnp.int32, length)
    allowed = (key_place[None, :] <= query_place[:, None])[None]
    peak = jnp.max(jnp.where(allowed, scores, -jnp.inf), axis=-1)
    exponent = jnp.where(allowed, jnp.exp(scores - peak[..., None]), 0.0)
    probs = exponent.astype(jnp.bfloat16)
    row_sum = jnp.sum(exponent, axis=-1)
    weighted = jnp.einsum("hqk,khd->hqd", probs, value_heads, preferred_element_type=jnp.float32)
    return (weighted / row_sum[..., None]).transpose(0, 2, 1).reshape(width, tok_rows).astype(
        jnp.bfloat16
    )


def local(
    queries, key_rows, values, code_first, code_second, book_first, book_second, scales, target
):
    parts = 2
    rows = scales.shape[0] // parts
    books = jnp.stack([book_first.T, book_second.T]).astype(jnp.float32)
    attended = attend(queries, key_rows, values)
    width, tok_rows = attended.shape
    pieces = lax.all_gather(attended, ("row", "tok"), axis=0)
    pieces = pieces.reshape(lax.axis_size("row"), lax.axis_size("tok"), width, tok_rows)
    gathered = pieces.transpose(0, 2, 1, 3).reshape(pieces.shape[0] * width, -1)
    tokens = gathered.shape[1]
    misfits, grad_scales, totals = [], [], []

    def finish(part, partial_value, codes, ahead):
        here = slice(part * rows, (part + 1) * rows)
        summed_out = lax.psum(partial_value, "col")
        if totals:
            wanted, totals[-1] = lax.optimization_barrier((target[:, here], totals[-1]))
        else:
            wanted = target[:, here]
        misfit = (summed_out - wanted.astype(jnp.float32)).astype(jnp.bfloat16)
        grad_scale = jnp.sum(misfit.astype(jnp.float32) * summed_out, axis=0)
        grad_scales.append(grad_scale / (scales[here] * tokens))
        next_value = None
        if ahead is not None:
            weight, misfit = lax.optimization_barrier((ahead, misfit))
            next_value = project(weight)
            misfit, next_value = lax.optimization_barrier((misfit, next_value))
        misfits.append(misfit)
        totals.append(bin_grads(gathered, misfit, codes, (scales[here] / tokens)[None]))
        return next_value

    def project(weight):
        return lax.dot_general(
            gathered, weight, (((0,), (0,)), ((), ())), preferred_element_type=jnp.float32
        )

    weight, codes = dequantize(code_first, code_second, books, scales[None], 0, parts)
    partial_value = project(weight)
    for part in range(parts):
        ahead = next_codes = None
        if part + 1 < parts:
            row_scales, partial_value = lax.optimization_barrier((scales[None], partial_value))
            ahead, next_codes = dequantize(
                code_first, code_second, books, row_scales, part + 1, parts
            )
        partial_value = finish(part, partial_value, codes, ahead)
        codes = next_codes
    return (jnp.concatenate(misfits, axis=1), jnp.concatenate(grad_scales), sum_books(totals))


def solution(mesh):
    in_specs = (
        P("tok", ("col", "row")),
        P("tok", ("col", "row")),
        P("tok", ("col", "row")),
        P(("row", "tok"), "col"),
        P(("row", "tok"), "col"),
        P(),
        P(),
        P(("row", "tok")),
        P(None, ("row", "tok")),
    )
    out_specs = (P(None, ("row", "tok")), P(("row", "tok")), P())
    return jax.shard_map(local, mesh=mesh, in_specs=in_specs, out_specs=out_specs, check_vma=False)
```

```python
import functools
import math

import jax
import jax.numpy as jnp
from jax import lax
from jax.experimental import pallas as pl
from jax.experimental.pallas import tpu as pltpu
from jax.sharding import PartitionSpec as P

HEAD_DIM = 128
ENTRIES = 256
GROUP = 8
LANES = 128
LOW = 8
HIGH = ENTRIES // LOW
OCTET = 8
VMEM_LIMIT = 48 * 1024 * 1024


def look_up(table, codes):
    place = codes & (LANES - 1)
    lower = jnp.take_along_axis(table[0], place, axis=1, mode="promise_in_bounds")
    upper = jnp.take_along_axis(table[1], place, axis=1, mode="promise_in_bounds")
    return jnp.where((codes & LANES) != 0, upper, lower)


def dequantize_kernel(first_ref, second_ref, books_ref, scales_ref, weight_ref, codes_ref):
    codes_ref[...] = (first_ref[...] + second_ref[...] * ENTRIES).T
    groups, rows = codes_ref.shape
    tables = [
        [books_ref[book, :, half * LANES : (half + 1) * LANES] for half in range(2)]
        for book in range(2)
    ]

    @pl.loop(0, groups // 2, unroll=16)
    def _(pair):
        parts = []
        for side in range(2):
            row = codes_ref[pl.ds(pair * 2 + side, 1), :]
            pieces = []
            for start in range(0, rows, LANES):
                codes = jnp.broadcast_to(row[:, start : start + LANES], (GROUP, LANES))
                unscaled = look_up(tables[0], codes) + look_up(tables[1], codes >> 8)
                pieces.append(unscaled * scales_ref[:, start : start + LANES])
            parts.append(jnp.concatenate(pieces, axis=1))
        rows16 = pl.ds(pl.multiple_of(pair * 16, 16), 16)
        weight_ref[rows16, :] = jnp.concatenate(parts, axis=0).astype(jnp.bfloat16)


def dequantize(code_first, code_second, books, scales, part, parts):
    groups = code_first.shape[1]
    rows = code_first.shape[0] // parts
    block = math.gcd(rows, 512)
    first = part * (rows // block)
    return pl.pallas_call(
        dequantize_kernel,
        grid=(groups // LANES, rows // block),
        in_specs=[
            pl.BlockSpec((block, LANES), lambda g, o: (first + o, g)),
            pl.BlockSpec((block, LANES), lambda g, o: (first + o, g)),
            pl.BlockSpec((2, GROUP, ENTRIES), lambda g, o: (0, 0, 0)),
            pl.BlockSpec((1, block), lambda g, o: (0, first + o)),
        ],
        out_specs=[
            pl.BlockSpec((LANES * GROUP, block), lambda g, o: (g, o)),
            pl.BlockSpec((LANES, block), lambda g, o: (g, o)),
        ],
        out_shape=[
            jax.ShapeDtypeStruct((groups * GROUP, rows), jnp.bfloat16),
            jax.ShapeDtypeStruct((groups, rows), jnp.int32),
        ],
        compiler_params=pltpu.CompilerParams(vmem_limit_bytes=VMEM_LIMIT),
        cost_estimate=pl.CostEstimate(
            flops=32 * rows * groups * GROUP,
            bytes_accessed=rows * groups * (12 + 2 * GROUP),
            transcendentals=0,
        ),
        name="dequantize",
    )(code_first, code_second, books, scales)


def bin_kernel(chunk, attended_ref, misfit_ref, codes_ref, scales_ref, total_ref, grad_ref):
    @pl.when(pl.program_id(0) == 0)
    def _():
        total_ref[...] = jnp.zeros_like(total_ref)

    rows = misfit_ref.shape[1]
    groups = codes_ref.shape[0]
    width = OCTET * GROUP

    @pl.loop(0, rows // chunk)
    def _(part):
        cols = pl.ds(pl.multiple_of(part * chunk, chunk), chunk)
        grad_ref[...] = (
            jnp.dot(
                attended_ref[...], misfit_ref[:, cols], preferred_element_type=jnp.float32
            )
            * scales_ref[:, cols]
        ).astype(jnp.bfloat16)

        @pl.loop(0, groups // OCTET, unroll=groups // OCTET)
        def _(octet):
            grad = grad_ref[pl.ds(pl.multiple_of(octet * width, width), width), :]
            places = lax.broadcasted_iota(jnp.int32, (HIGH, chunk), 0).astype(jnp.bfloat16)
            lines = [codes_ref[pl.ds(octet * OCTET + g, 1), cols] for g in range(OCTET)]
            for book in range(2):
                own = [(line >> (8 * book)) & (ENTRIES - 1) for line in lines]
                low = jnp.concatenate(
                    [jnp.broadcast_to(code & (LOW - 1), (GROUP, chunk)) for code in own], axis=0
                ).astype(jnp.bfloat16)
                left = jnp.concatenate(
                    [
                        jnp.where(low == jnp.bfloat16(k), grad, jnp.bfloat16(0))
                        for k in range(LOW)
                    ],
                    axis=0,
                )
                right = jnp.concatenate(
                    [
                        jnp.where(
                            jnp.broadcast_to(code // LOW, (HIGH, chunk)).astype(jnp.bfloat16)
                            == places,
                            jnp.bfloat16(1),
                            jnp.bfloat16(0),
                        )
                        for code in own
                    ],
                    axis=0,
                )
                total_ref[book] += lax.dot_general(
                    left, right, (((1,), (1,)), ((), ())), preferred_element_type=jnp.float32
                )


def bin_grads(attended, misfit, codes, scales):
    groups, rows = codes.shape
    tokens = misfit.shape[0]
    block = math.gcd(groups, 64)
    chunk = math.gcd(rows, 1024)
    return pl.pallas_call(
        functools.partial(bin_kernel, chunk),
        grid=(groups // block,),
        in_specs=[
            pl.BlockSpec((block * GROUP, tokens), lambda g: (g, 0)),
            pl.BlockSpec((tokens, rows), lambda g: (0, 0)),
            pl.BlockSpec((block, rows), lambda g: (g, 0)),
            pl.BlockSpec((1, rows), lambda g: (0, 0)),
        ],
        out_specs=pl.BlockSpec(
            (2, LOW * OCTET * GROUP, OCTET * HIGH), lambda g: (0, 0, 0)
        ),
        out_shape=jax.ShapeDtypeStruct((2, LOW * OCTET * GROUP, OCTET * HIGH), jnp.float32),
        scratch_shapes=[pltpu.VMEM((block * GROUP, chunk), jnp.bfloat16)],
        compiler_params=pltpu.CompilerParams(vmem_limit_bytes=VMEM_LIMIT),
        cost_estimate=pl.CostEstimate(
            flops=4 * rows * groups * LOW * GROUP * OCTET * HIGH,
            bytes_accessed=rows * groups * 4,
            transcendentals=0,
        ),
        name="bin_grads",
    )(attended, misfit, codes, scales)

def fold_book(total):
    groups_at = lax.broadcasted_iota(jnp.int32, total.shape, 0) // GROUP % OCTET
    lanes_at = lax.broadcasted_iota(jnp.int32, total.shape, 1) // HIGH
    kept = jnp.where(groups_at == lanes_at, total, 0.0)
    kept = jnp.sum(kept.reshape(LOW, OCTET, GROUP, OCTET * HIGH), axis=1)
    kept = kept.reshape(LOW * GROUP, OCTET * HIGH)
    kept = kept[:, :LANES] + kept[:, LANES:]
    kept = kept + pltpu.roll(kept, 2 * HIGH, 1)
    return kept + pltpu.roll(kept, HIGH, 1)


def sum_kernel(axes, *refs):
    count = len(axes)
    total_refs, out_ref = refs[: -3 * count - 1], refs[-3 * count - 1]
    slots, sends, arrivals = (
        refs[-3 * count : -2 * count],
        refs[-2 * count : -count],
        refs[-count:],
    )
    barrier = pltpu.get_barrier_semaphore()
    peers = 0
    for name, size in axes:
        me = lax.axis_index(name)
        for ahead in range(1, size):
            pl.semaphore_signal(
                barrier,
                inc=1,
                device_id={name: lax.rem(me + ahead, size)},
                device_id_type=pl.DeviceIdType.MESH,
            )
            peers += 1
    folded = []
    for book in range(2):
        total = total_refs[0][book]
        for ref in total_refs[1:]:
            total = total + ref[book]
        folded.append(fold_book(total))
    lane = lax.broadcasted_iota(jnp.int32, folded[0].shape, 1)
    current = jnp.where(lane < HIGH, folded[0], folded[1])
    pl.semaphore_wait(barrier, peers)
    for stage, (name, size) in enumerate(axes):
        me = lax.axis_index(name)
        slots[stage][me] = current
        copies = []
        for ahead in range(1, size):
            copy = pltpu.make_async_remote_copy(
                src_ref=slots[stage].at[me],
                dst_ref=slots[stage].at[me],
                send_sem=sends[stage].at[ahead],
                recv_sem=arrivals[stage].at[ahead],
                device_id={name: lax.rem(me + ahead, size)},
                device_id_type=pl.DeviceIdType.MESH,
            )
            copy.start()
            copies.append(copy)
        for copy in copies:
            copy.wait()
        current = slots[stage][0]
        for place in range(1, size):
            current = current + slots[stage][place]
    out_ref[...] = current


def sum_books(totals):
    axes = [(name, lax.axis_size(name)) for name in ("col", "row", "tok")]
    shape = (LOW * GROUP, LANES)
    summed = pl.pallas_call(
        functools.partial(sum_kernel, axes),
        in_specs=[pl.BlockSpec(memory_space=pltpu.VMEM)] * len(totals),
        out_specs=pl.BlockSpec(memory_space=pltpu.VMEM),
        out_shape=jax.ShapeDtypeStruct(shape, jnp.float32),
        scratch_shapes=[pltpu.VMEM((size, *shape), jnp.float32) for _, size in axes]
        + [pltpu.SemaphoreType.DMA((size,)) for _, size in axes] * 2,
        compiler_params=pltpu.CompilerParams(
            collective_id=0, has_side_effects=True, vmem_limit_bytes=VMEM_LIMIT
        ),
        name="sum_books",
    )(*totals)
    split = summed[:, : 2 * HIGH].reshape(LOW, GROUP, 2, HIGH)
    return split.transpose(2, 3, 0, 1).reshape(2, ENTRIES, GROUP)


def attend(queries, key_rows, values):
    tok_rows, width = queries.shape
    heads_here = width // HEAD_DIM
    query_heads = queries.reshape(tok_rows, heads_here, HEAD_DIM)
    query_place = lax.axis_index("tok") * tok_rows + lax.iota(jnp.int32, tok_rows)
    key_piece = lax.all_gather(key_rows, "tok", axis=0, tiled=True)
    value_piece = lax.all_gather(values, "tok", axis=0, tiled=True)
    length = key_piece.shape[0]
    key_heads = key_piece.reshape(length, heads_here, HEAD_DIM)
    value_heads = value_piece.reshape(length, heads_here, HEAD_DIM)
    scores = jnp.einsum(
        "qhd,khd->hqk", query_heads, key_heads, preferred_element_type=jnp.float32
    ) / math.sqrt(HEAD_DIM)
    key_place = lax.iota(jnp.int32, length)
    allowed = (key_place[None, :] <= query_place[:, None])[None]
    peak = jnp.max(jnp.where(allowed, scores, -jnp.inf), axis=-1)
    exponent = jnp.where(allowed, jnp.exp(scores - peak[..., None]), 0.0)
    probs = exponent.astype(jnp.bfloat16)
    row_sum = jnp.sum(exponent, axis=-1)
    weighted = jnp.einsum("hqk,khd->hqd", probs, value_heads, preferred_element_type=jnp.float32)
    return (weighted / row_sum[..., None]).transpose(0, 2, 1).reshape(width, tok_rows).astype(
        jnp.bfloat16
    )


def local(
    queries, key_rows, values, code_first, code_second, book_first, book_second, scales, target
):
    parts = 2
    rows = scales.shape[0] // parts
    books = jnp.stack([book_first.T, book_second.T]).astype(jnp.float32)
    attended = attend(queries, key_rows, values)
    width, tok_rows = attended.shape
    pieces = lax.all_gather(attended, ("row", "tok"), axis=0)
    pieces = pieces.reshape(lax.axis_size("row"), lax.axis_size("tok"), width, tok_rows)
    gathered = pieces.transpose(0, 2, 1, 3).reshape(pieces.shape[0] * width, -1)
    tokens = gathered.shape[1]
    misfits, grad_scales, totals = [], [], []

    def finish(part, partial_value, codes, ahead):
        here = slice(part * rows, (part + 1) * rows)
        summed_out = lax.psum(partial_value, "col")
        if totals:
            wanted, totals[-1] = lax.optimization_barrier((target[:, here], totals[-1]))
        else:
            wanted = target[:, here]
        misfit = (summed_out - wanted.astype(jnp.float32)).astype(jnp.bfloat16)
        grad_scale = jnp.sum(misfit.astype(jnp.float32) * summed_out, axis=0)
        grad_scales.append(grad_scale / (scales[here] * tokens))
        next_value = None
        if ahead is not None:
            weight, misfit = lax.optimization_barrier((ahead, misfit))
            next_value = project(weight)
            misfit, next_value = lax.optimization_barrier((misfit, next_value))
        misfits.append(misfit)
        totals.append(bin_grads(gathered, misfit, codes, (scales[here] / tokens)[None]))
        return next_value

    def project(weight):
        return lax.dot_general(
            gathered, weight, (((0,), (0,)), ((), ())), preferred_element_type=jnp.float32
        )

    weight, codes = dequantize(code_first, code_second, books, scales[None], 0, parts)
    partial_value = project(weight)
    for part in range(parts):
        ahead = next_codes = None
        if part + 1 < parts:
            row_scales, partial_value = lax.optimization_barrier((scales[None], partial_value))
            ahead, next_codes = dequantize(
                code_first, code_second, books, row_scales, part + 1, parts
            )
        partial_value = finish(part, partial_value, codes, ahead)
        codes = next_codes
    return (jnp.concatenate(misfits, axis=1), jnp.concatenate(grad_scales), sum_books(totals))


def solution(mesh):
    in_specs = (
        P("tok", ("col", "row")),
        P("tok", ("col", "row")),
        P("tok", ("col", "row")),
        P(("row", "tok"), "col"),
        P(("row", "tok"), "col"),
        P(),
        P(),
        P(("row", "tok")),
        P(None, ("row", "tok")),
    )
    out_specs = (P(None, ("row", "tok")), P(("row", "tok")), P())
    return jax.shard_map(local, mesh=mesh, in_specs=in_specs, out_specs=out_specs, check_vma=False)
```
